32 devices in a mesh: fsdp: 16 (over z, y, x), tp: 2 (over core).
Axes of the slice: x: 2, y: 2, z: 4, core: 2. Of those that a mesh axis runs over, the one named last changes fastest.
Arguments:
- gradient: bfloat16 [2, 8192, 8192], P(None, 'fsdp', 'tp'), may hold values from -2764800 to 2764800
- momentum: float32 [2, 8192, 8192], P(None, 'fsdp', 'tp'), may hold values from -36 to 36
- right_basis_old: float32 [2, 512, 8192], P(None, 'fsdp', 'tp'), may hold values from -6 to 6
- token_counts: int32 [32], P(('fsdp', 'tp')), may hold values from 400 to 6397, as said below
Outputs:
- momentum_corrected: float32 [2, 8192, 8192], P(None, 'fsdp', 'tp')
- direction: float32 [2, 8192, 8192], P(None, 'fsdp', 'tp')
- right_basis_new: float32 [2, 512, 8192], P(None, 'fsdp', 'tp')
The draws below stay inside these ranges and needn't reach their ends.
Inputs may be any that keep to these rules, and one draw needn't show every extreme that they name: `token_counts`: each device's count; the first entry is 400.
All inputs are finite; a program needn't handle non-finite values.
Results may differ from the reference program's by a relative error of at most 0.0003.
Values sent between devices are 32-bit elements; how exact they have to be, the bound alone decides.
A program may use at most 256 MiB of HBM per device.

```python
import math
import jax
import jax.numpy as jnp
from jax import lax

MODEL_WIDTH = 8192
UPDATE_RANK = 512
MATS = 2
N_FSDP = 16
N_TP = 2


def column_scales(key):
    key = jax.random.fold_in(key, 101)
    spread = jnp.exp(jax.random.uniform(key, (MATS, 1, MODEL_WIDTH), jnp.float32, 0.0, math.log(10.0)))
    rising = 1.0 + 2.0 * jnp.arange(MODEL_WIDTH, dtype=jnp.float32) / (MODEL_WIDTH - 1)
    return 0.3 * spread * rising


def draw_momentum(key, part):
    scales = column_scales(key)
    key = jax.random.fold_in(key, 7)
    noise = jax.random.truncated_normal(key, -4.0, 4.0, (MATS, MODEL_WIDTH, MODEL_WIDTH), jnp.float32)
    return (noise * scales).astype(jnp.float32)


def draw_gradient(key, part):
    scales = column_scales(key)
    key = jax.random.fold_in(key, 11)
    noise = jax.random.truncated_normal(key, -4.0, 4.0, (MATS, MODEL_WIDTH, MODEL_WIDTH), jnp.float32)
    return (noise * scales * (2400.0 * N_FSDP * N_TP)).astype(jnp.bfloat16)


def draw_token_counts(key, part):
    key = jax.random.fold_in(key, 3)
    count = N_FSDP * N_TP
    draws = jax.random.randint(key, (count,), 0, 2000, jnp.int32)
    index = jnp.arange(count, dtype=jnp.int32)
    draws = jnp.where(index == 0, 0, jnp.where(index == count - 1, 1999, draws))
    return (400 + draws + 2 * draws * index // max(count - 1, 1)).astype(jnp.int32)


def level_of(own_key, dims, cuts, low, top_value):
    level, own = 1.0, jax.random.fold_in(own_key, 6)
    for dim, shards_of in cuts:
        steps = jnp.exp(jax.random.uniform(jax.random.fold_in(own, dim), (shards_of,), jnp.float32, low / len(cuts), top_value / len(cuts)))
        level = level * jnp.repeat(steps, dims[dim] // shards_of).reshape([-1 if axis == dim else 1 for axis in range(len(dims))])
    return level


def gaussian(rng, shape, scale, most, cuts=(), kind=jnp.bfloat16):
    entries = jax.random.normal(rng, shape, jnp.float32) * scale
    if len(cuts) > 0:
        entries = level_of(rng, shape, cuts, -0.22, 0.18) * entries
    return jnp.clip(entries, min=-most, max=most).astype(kind)


def setup_inputs(seed: int = 0) -> dict:
    seeds = jax.random.split(jax.random.key(seed), 5)
    return {
        "gradient": draw_gradient(jax.random.fold_in(seeds[4], 71), 0),
        "momentum": draw_momentum(jax.random.fold_in(seeds[4], 71), 0),
        "right_basis_old": gaussian(seeds[2], (MATS, UPDATE_RANK, MODEL_WIDTH), 1.0, 6.0, ((1, 16), (2, 2)), jnp.float32),
        "token_counts": draw_token_counts(jax.random.fold_in(seeds[4], 71), 0),
    }


epsilon = 1e-06
retained_fraction = 0.05
top_precision = lax.Precision.HIGHEST

def orthonormalize(factor, momentum_product):
    return jax.scipy.linalg.solve_triangular(factor, momentum_product.T, lower=True).T

def reference(gradient, momentum, right_basis_old, token_counts):
    token_total = jnp.sum(token_counts.astype(jnp.float32))
    momentum_store = momentum + gradient.astype(jnp.float32) / token_total
    momentum_product = jnp.einsum('gyp,gep->gye', momentum_store, right_basis_old, precision=top_precision)
    inner_products = jnp.einsum('eut,eug->etg', momentum_product, momentum_product, precision=top_precision)
    factor = jnp.linalg.cholesky(inner_products)
    orthogonal_factor = jax.vmap(orthonormalize)(factor, momentum_product)
    product_total = jnp.einsum('kwd,kwy->kdy', orthogonal_factor, momentum_store, precision=top_precision)
    row_rms = jnp.sqrt(lax.optimization_barrier(jnp.mean(product_total * product_total, axis=2)) + epsilon)
    right_basis_new = product_total / row_rms[:, :, None]
    momentum_corrected = momentum_store - retained_fraction * jnp.einsum('wlj,wja->wla', orthogonal_factor, product_total, precision=top_precision)
    direction = math.sqrt(MODEL_WIDTH / UPDATE_RANK) * jnp.einsum('wlj,wja->wla', orthogonal_factor, right_basis_new, precision=top_precision)
    return (momentum_corrected, direction, right_basis_new)
```

```python
import functools
import math

import jax
import jax.numpy as jnp
from jax import lax
from jax.experimental import pallas as pl
from jax.experimental.pallas import tpu as pltpu
from jax.sharding import PartitionSpec as P

epsilon = 1e-06
retained_fraction = 0.05
top_precision = lax.Precision.HIGHEST
good_precision = lax.Precision.HIGH
MESH = pl.DeviceIdType.MESH
PANEL = 128


def place_of(device, n):
    if n != 16:
        return device
    z, y, x = device // 4, (device // 2) % 2, device % 2
    column = 3 * y + x - 2 * x * y
    along = z + (column % 2) * (3 - 2 * z)
    return column * 4 + along


def device_at(place, n):
    if n != 16:
        return place
    column, along = place // 4, place % 4
    z = along + (column % 2) * (3 - 2 * along)
    x, y = ((column + 1) // 2) % 2, column // 2
    return z * 4 + y * 2 + x


def scatter_kernel(n, halves, terms, out, slots, send_sem, recv_sem):
    me = lax.axis_index("fsdp")
    place = place_of(me, n)
    right = device_at((place + 1) % n, n)
    left = device_at((place + n - 1) % n, n)
    rows, width = out.shape[1], out.shape[2] // halves

    barrier = pltpu.get_barrier_semaphore()
    for neighbour in (left, right):
        pl.semaphore_signal(barrier, inc=1, device_id={"fsdp": neighbour}, device_id_type=MESH)
    pl.semaphore_wait(barrier, 2)

    streams = [(mat, half) for half in range(halves) for mat in range(2)]

    def rows_at(mat, step):
        if mat == 0:
            block = device_at((place + 2 * n - 1 - step) % n, n)
        else:
            block = device_at((place + 1 + step) % n, n)
        return pl.ds(pl.multiple_of(block * rows, rows), rows)

    def copy(mat, half, step, source):
        columns = pl.ds(half * width, width)
        stream = mat * halves + half
        return pltpu.make_async_remote_copy(
            src_ref=source,
            dst_ref=slots.at[step, mat, :, columns],
            send_sem=send_sem.at[stream, step],
            recv_sem=recv_sem.at[stream, step],
            device_id={"fsdp": right if mat == 0 else left},
            device_id_type=MESH,
        )

    def held(mat, half, step):
        return slots.at[step, mat, :, pl.ds(half * width, width)]

    for mat, half in streams:
        copy(mat, half, 0, terms.at[mat, rows_at(mat, 0), pl.ds(half * width, width)]).start()

    def step_body(step, carry):
        for mat, half in streams:
            columns = pl.ds(half * width, width)
            before = held(mat, half, step - 1)
            copy(mat, half, step - 1, before).wait_recv()
            slots[step - 1, mat, :, columns] = (
                slots[step - 1, mat, :, columns] + terms[mat, rows_at(mat, step), columns]
            )
            copy(mat, half, step, before).start()
        return carry

    lax.fori_loop(1, n - 1, step_body, 0)
    for mat, half in streams:
        columns = pl.ds(half * width, width)
        copy(mat, half, n - 2, held(mat, half, n - 2)).wait_recv()
        out[mat, :, columns] = slots[n - 2, mat, :, columns] + terms[mat, rows_at(mat, n - 1), columns]

    def drain(step, carry):
        for mat, half in streams:
            copy(mat, half, step, held(mat, half, step)).wait_send()
        return carry

    lax.fori_loop(0, n - 1, drain, 0)


def ring_scatter(terms, n):
    mats, rank, width = terms.shape
    rows, halves = rank // n, 2
    return pl.pallas_call(
        functools.partial(scatter_kernel, n, halves),
        out_shape=jax.ShapeDtypeStruct((mats, rows, width), jnp.float32),
        in_specs=[pl.BlockSpec(memory_space=pltpu.VMEM)],
        out_specs=pl.BlockSpec(memory_space=pltpu.VMEM),
        scratch_shapes=[
            pltpu.VMEM((n - 1, mats, rows, width), jnp.float32),
            pltpu.SemaphoreType.DMA((2 * halves, n - 1)),
            pltpu.SemaphoreType.DMA((2 * halves, n - 1)),
        ],
        cost_estimate=pl.CostEstimate(
            flops=terms.size, bytes_accessed=terms.size * 40, transcendentals=0
        ),
        compiler_params=pltpu.CompilerParams(
            collective_id=0, has_side_effects=True, vmem_limit_bytes=48 * 1024 * 1024
        ),
        name="ring_scatter",
    )(terms)


def dot_top(a, b, contract):
    return lax.dot_general(
        a, b, (contract, ((), ())), precision=top_precision, preferred_element_type=jnp.float32
    )


def factor_panels(panels):
    tiles = PANEL // 8
    row_ids = lax.broadcasted_iota(jnp.int32, (8, PANEL), 0)
    lane_ids = lax.broadcasted_iota(jnp.int32, (8, PANEL), 1)
    state = []
    for panel in panels:
        a = [panel[8 * i : 8 * i + 8, :] for i in range(tiles)]
        x = [jnp.where(lane_ids == row_ids + 8 * i, 1.0, 0.0).astype(jnp.float32) for i in range(tiles)]
        state.append((a, x))
    for j in range(PANEL):
        b, r = j // 8, j % 8
        for a, x in state:
            pivot = jnp.broadcast_to(a[b][r : r + 1, j : j + 1], (1, PANEL))
            scale = lax.rsqrt(pivot)
            scale = scale * (1.5 - 0.5 * pivot * scale * scale)
            row_a = a[b][r : r + 1, :] * scale
            row_x = x[b][r : r + 1, :] * scale
            scaled_a, scaled_x = row_a * scale, row_x * scale
            for i in range(b, tiles):
                if i == b and r == 7:
                    continue
                column = jnp.broadcast_to(a[i][:, j : j + 1], (8, PANEL))
                if i == b:
                    column = jnp.where(row_ids > r, column, 0.0)
                a[i] = a[i] - column * scaled_a
                x[i] = x[i] - column * scaled_x
            a[b] = jnp.where(row_ids == r, row_a, a[b])
            x[b] = jnp.where(row_ids == r, row_x, x[b])
    return [jnp.concatenate(x, axis=0) for _, x in state]


def factor_kernel(gram, inverse, work):
    mats, rank = gram.shape[0], gram.shape[1]
    row_ids = lax.broadcasted_iota(jnp.int32, (rank, rank), 0)
    lane_ids = lax.broadcasted_iota(jnp.int32, (rank, rank), 1)
    for m in range(mats):
        work[m] = gram[m]
        inverse[m] = jnp.where(row_ids == lane_ids, 1.0, 0.0).astype(jnp.float32)

    def diagonal(k, carry):
        at = pl.multiple_of(k * PANEL, PANEL)
        here = pl.ds(at, PANEL)
        lower = factor_panels([work[m, here, here] for m in range(mats)])
        for m in range(mats):
            solved = dot_top(lower[m], work[m, here, :], ((1,), (0,)))
            solved_inverse = dot_top(lower[m], inverse[m, here, :], ((1,), (0,)))
            lanes = lax.broadcasted_iota(jnp.int32, solved.shape, 1)
            below = jnp.where(lanes >= at + PANEL, solved, 0.0)
            work[m] = work[m] - dot_top(below, below, ((0,), (0,)))
            inverse[m] = inverse[m] - dot_top(below, solved_inverse, ((0,), (0,)))
            inverse[m, here, :] = solved_inverse
        return carry

    lax.fori_loop(0, rank // PANEL, diagonal, 0)


def inverse_factor(gram):
    return pl.pallas_call(
        factor_kernel,
        out_shape=jax.ShapeDtypeStruct(gram.shape, jnp.float32),
        in_specs=[pl.BlockSpec(memory_space=pltpu.VMEM)],
        out_specs=pl.BlockSpec(memory_space=pltpu.VMEM),
        scratch_shapes=[pltpu.VMEM(gram.shape, jnp.float32)],
        cost_estimate=pl.CostEstimate(flops=80_000_000_000, bytes_accessed=4 << 20, transcendentals=0),
        compiler_params=pltpu.CompilerParams(vmem_limit_bytes=40 * 1024 * 1024),
        name="inverse_factor",
    )(gram)


def per_device(n, gradient, momentum, right_basis_old, token_counts):
    mats = momentum.shape[0]
    token_total = lax.psum(jnp.sum(token_counts.astype(jnp.float32)), ("fsdp", "tp"))
    width = momentum.shape[2] * lax.axis_size("tp")
    rank = right_basis_old.shape[1] * n

    basis = lax.all_gather(right_basis_old, "fsdp", axis=1, tiled=True)
    store = momentum + gradient.astype(jnp.float32) / token_total
    projected = lax.psum(jnp.einsum("mij,mkj->mik", store, basis, precision=top_precision), "tp")
    gram = lax.psum(jnp.einsum("mut,mug->mtg", projected, projected, precision=top_precision), "fsdp")
    terms = jnp.einsum("mut,muc->mtc", projected, store, precision=good_precision)
    own_rows = ring_scatter(terms, n)
    inverse = inverse_factor(gram)
    whole = lax.all_gather(own_rows, "fsdp", axis=1, tiled=True)
    orthonormal = jnp.einsum("mut,mrt->mur", projected, inverse, precision=top_precision)
    reduced = jnp.einsum("mrt,mtc->mrc", inverse, whole, precision=good_precision)
    squares = lax.psum(jnp.sum(reduced * reduced, axis=2), "tp")
    row_rms = jnp.sqrt(squares / width + epsilon)
    corrected = store - retained_fraction * jnp.einsum(
        "mur,mrc->muc", orthonormal, reduced, precision=good_precision
    )
    scaled = orthonormal * (math.sqrt(width / rank) / row_rms)[:, None, :]
    direction = jnp.einsum("mur,mrc->muc", scaled, reduced, precision=good_precision)
    rows = rank // n
    first = lax.axis_index("fsdp") * rows
    right_basis_new = (
        lax.dynamic_slice_in_dim(reduced, first, rows, 1)
        / lax.dynamic_slice_in_dim(row_rms, first, rows, 1)[:, :, None]
    )
    return (corrected, direction, right_basis_new)


def solution(mesh):
    spec = P(None, "fsdp", "tp")
    return jax.shard_map(
        functools.partial(per_device, mesh.shape["fsdp"]),
        mesh=mesh,
        in_specs=(spec, spec, spec, P(("fsdp", "tp"))),
        out_specs=(spec, spec, spec),
        check_vma=False,
    )
```

```python
import functools
import math

import jax
import jax.numpy as jnp
from jax import lax
from jax.experimental import pallas as pl
from jax.experimental.pallas import tpu as pltpu
from jax.sharding import PartitionSpec as P

epsilon = 1e-06
retained_fraction = 0.05
top_precision = lax.Precision.HIGHEST
good_precision = lax.Precision.HIGH
MESH = pl.DeviceIdType.MESH
PANEL = 128


def place_of(device, n):
    if n != 16:
        return device
    z, y, x = device // 4, (device // 2) % 2, device % 2
    column = 3 * y + x - 2 * x * y
    along = z + (column % 2) * (3 - 2 * z)
    return column * 4 + along


def device_at(place, n):
    if n != 16:
        return place
    column, along = place // 4, place % 4
    z = along + (column % 2) * (3 - 2 * along)
    x, y = ((column + 1) // 2) % 2, column // 2
    return z * 4 + y * 2 + x


def scatter_kernel(n, halves, terms, out, slots, send_sem, recv_sem):
    me = lax.axis_index("fsdp")
    place = place_of(me, n)
    right = device_at((place + 1) % n, n)
    left = device_at((place + n - 1) % n, n)
    rows, width = out.shape[1], out.shape[2] // halves

    barrier = pltpu.get_barrier_semaphore()
    for neighbour in (left, right):
        pl.semaphore_signal(barrier, inc=1, device_id={"fsdp": neighbour}, device_id_type=MESH)
    pl.semaphore_wait(barrier, 2)

    streams = [(mat, half) for half in range(halves) for mat in range(2)]

    def rows_at(mat, step):
        if mat == 0:
            block = device_at((place + 2 * n - 1 - step) % n, n)
        else:
            block = device_at((place + 1 + step) % n, n)
        return pl.ds(pl.multiple_of(block * rows, rows), rows)

    def copy(mat, half, step, source):
        columns = pl.ds(half * width, width)
        stream = mat * halves + half
        return pltpu.make_async_remote_copy(
            src_ref=source,
            dst_ref=slots.at[step, mat, :, columns],
            send_sem=send_sem.at[stream, step],
            recv_sem=recv_sem.at[stream, step],
            device_id={"fsdp": right if mat == 0 else left},
            device_id_type=MESH,
        )

    def held(mat, half, step):
        return slots.at[step, mat, :, pl.ds(half * width, width)]

    for mat, half in streams:
        copy(mat, half, 0, terms.at[mat, rows_at(mat, 0), pl.ds(half * width, width)]).start()

    def step_body(step, carry):
        for mat, half in streams:
            columns = pl.ds(half * width, width)
            before = held(mat, half, step - 1)
            copy(mat, half, step - 1, before).wait_recv()
            slots[step - 1, mat, :, columns] = (
                slots[step - 1, mat, :, columns] + terms[mat, rows_at(mat, step), columns]
            )
            copy(mat, half, step, before).start()
        return carry

    lax.fori_loop(1, n - 1, step_body, 0)
    for mat, half in streams:
        columns = pl.ds(half * width, width)
        copy(mat, half, n - 2, held(mat, half, n - 2)).wait_recv()
        out[mat, :, columns] = slots[n - 2, mat, :, columns] + terms[mat, rows_at(mat, n - 1), columns]

    def drain(step, carry):
        for mat, half in streams:
            copy(mat, half, step, held(mat, half, step)).wait_send()
        return carry

    lax.fori_loop(0, n - 1, drain, 0)


def ring_scatter(terms, n):
    mats, rank, width = terms.shape
    rows, halves = rank // n, 4
    return pl.pallas_call(
        functools.partial(scatter_kernel, n, halves),
        out_shape=jax.ShapeDtypeStruct((mats, rows, width), jnp.float32),
        in_specs=[pl.BlockSpec(memory_space=pltpu.VMEM)],
        out_specs=pl.BlockSpec(memory_space=pltpu.VMEM),
        scratch_shapes=[
            pltpu.VMEM((n - 1, mats, rows, width), jnp.float32),
            pltpu.SemaphoreType.DMA((2 * halves, n - 1)),
            pltpu.SemaphoreType.DMA((2 * halves, n - 1)),
        ],
        cost_estimate=pl.CostEstimate(
            flops=terms.size, bytes_accessed=terms.size * 40, transcendentals=0
        ),
        compiler_params=pltpu.CompilerParams(
            collective_id=0, has_side_effects=True, vmem_limit_bytes=48 * 1024 * 1024
        ),
        name="ring_scatter",
    )(terms)


def dot_top(a, b, contract):
    return lax.dot_general(
        a, b, (contract, ((), ())), precision=top_precision, preferred_element_type=jnp.float32
    )


def factor_panels(panels):
    tiles = PANEL // 8
    row_ids = lax.broadcasted_iota(jnp.int32, (8, PANEL), 0)
    lane_ids = lax.broadcasted_iota(jnp.int32, (8, PANEL), 1)
    state = []
    for panel in panels:
        a = [panel[8 * i : 8 * i + 8, :] for i in range(tiles)]
        x = [jnp.where(lane_ids == row_ids + 8 * i, 1.0, 0.0).astype(jnp.float32) for i in range(tiles)]
        state.append((a, x))
    for j in range(PANEL):
        b, r = j // 8, j % 8
        for a, x in state:
            pivot = jnp.broadcast_to(a[b][r : r + 1, j : j + 1], (1, PANEL))
            scale = lax.rsqrt(pivot)
            scale = scale * (1.5 - 0.5 * pivot * scale * scale)
            row_a = a[b][r : r + 1, :] * scale
            row_x = x[b][r : r + 1, :] * scale
            scaled_a, scaled_x = row_a * scale, row_x * scale
            for i in range(b, tiles):
                if i == b and r == 7:
                    continue
                column = jnp.broadcast_to(a[i][:, j : j + 1], (8, PANEL))
                if i == b:
                    column = jnp.where(row_ids > r, column, 0.0)
                a[i] = a[i] - column * scaled_a
                x[i] = x[i] - column * scaled_x
            a[b] = jnp.where(row_ids == r, row_a, a[b])
            x[b] = jnp.where(row_ids == r, row_x, x[b])
    return [jnp.concatenate(x, axis=0) for _, x in state]


def factor_kernel(gram, inverse, work):
    mats, rank = gram.shape[0], gram.shape[1]
    row_ids = lax.broadcasted_iota(jnp.int32, (rank, rank), 0)
    lane_ids = lax.broadcasted_iota(jnp.int32, (rank, rank), 1)
    for m in range(mats):
        work[m] = gram[m]
        inverse[m] = jnp.where(row_ids == lane_ids, 1.0, 0.0).astype(jnp.float32)

    def diagonal(k, carry):
        at = pl.multiple_of(k * PANEL, PANEL)
        here = pl.ds(at, PANEL)
        lower = factor_panels([work[m, here, here] for m in range(mats)])
        for m in range(mats):
            solved = dot_top(lower[m], work[m, here, :], ((1,), (0,)))
            solved_inverse = dot_top(lower[m], inverse[m, here, :], ((1,), (0,)))
            lanes = lax.broadcasted_iota(jnp.int32, solved.shape, 1)
            below = jnp.where(lanes >= at + PANEL, solved, 0.0)
            work[m] = work[m] - dot_top(below, below, ((0,), (0,)))
            inverse[m] = inverse[m] - dot_top(below, solved_inverse, ((0,), (0,)))
            inverse[m, here, :] = solved_inverse
        return carry

    lax.fori_loop(0, rank // PANEL, diagonal, 0)


def inverse_factor(gram):
    return pl.pallas_call(
        factor_kernel,
        out_shape=jax.ShapeDtypeStruct(gram.shape, jnp.float32),
        in_specs=[pl.BlockSpec(memory_space=pltpu.VMEM)],
        out_specs=pl.BlockSpec(memory_space=pltpu.VMEM),
        scratch_shapes=[pltpu.VMEM(gram.shape, jnp.float32)],
        cost_estimate=pl.CostEstimate(flops=80_000_000_000, bytes_accessed=4 << 20, transcendentals=0),
        compiler_params=pltpu.CompilerParams(vmem_limit_bytes=40 * 1024 * 1024),
        name="inverse_factor",
    )(gram)


def per_device(n, gradient, momentum, right_basis_old, token_counts):
    mats = momentum.shape[0]
    token_total = lax.psum(jnp.sum(token_counts.astype(jnp.float32)), ("fsdp", "tp"))
    width = momentum.shape[2] * lax.axis_size("tp")
    rank = right_basis_old.shape[1] * n

    basis = lax.all_gather(right_basis_old, "fsdp", axis=1, tiled=True)
    store = momentum + gradient.astype(jnp.float32) / token_total
    projected = lax.psum(jnp.einsum("mij,mkj->mik", store, basis, precision=good_precision), "tp")
    gram = lax.psum(jnp.einsum("mut,mug->mtg", projected, projected, precision=top_precision), "fsdp")
    terms = jnp.einsum("mut,muc->mtc", projected, store, precision=good_precision)
    own_rows = ring_scatter(terms, n)
    inverse = inverse_factor(gram)
    whole = lax.all_gather(own_rows, "fsdp", axis=1, tiled=True)
    orthonormal = jnp.einsum("mut,mrt->mur", projected, inverse, precision=top_precision)
    reduced = jnp.einsum("mrt,mtc->mrc", inverse, whole, precision=good_precision)
    squares = lax.psum(jnp.sum(reduced * reduced, axis=2), "tp")
    row_rms = jnp.sqrt(squares / width + epsilon)
    corrected = store - retained_fraction * jnp.einsum(
        "mur,mrc->muc", orthonormal, reduced, precision=good_precision
    )
    scaled = orthonormal * (math.sqrt(width / rank) / row_rms)[:, None, :]
    direction = jnp.einsum("mur,mrc->muc", scaled, reduced, precision=good_precision)
    rows = rank // n
    first = lax.axis_index("fsdp") * rows
    right_basis_new = (
        lax.dynamic_slice_in_dim(reduced, first, rows, 1)
        / lax.dynamic_slice_in_dim(row_rms, first, rows, 1)[:, :, None]
    )
    return (corrected, direction, right_basis_new)


def solution(mesh):
    spec = P(None, "fsdp", "tp")
    return jax.shard_map(
        functools.partial(per_device, mesh.shape["fsdp"]),
        mesh=mesh,
        in_specs=(spec, spec, spec, P(("fsdp", "tp"))),
        out_specs=(spec, spec, spec),
        check_vma=False,
    )
```
